256 devices in a mesh: blk: 64 (over z, x, y_lo), probe: 4 (over y_hi, core).
Axes of the slice: x: 4, y: 4 (y_hi: 2, y_lo: 2; y = y_hi * 2 + y_lo), z: 8, core: 2. Of those that a mesh axis runs over, the one named last changes fastest.
Arguments:
- points: float32 [8, 40960], P(None, ('blk', 'probe')), may hold values from -6 to 6
- targets: float32 [40960], P('blk'), may hold values from -12 to 12
- signs: int32 [15, 40960], P(None, 'blk'), may hold values from 0 to 1
Outputs:
- solution: float32 [16, 40960], P('probe', 'blk')
- residual: float32 [16, 40960], P('probe', 'blk')
- direction: float32 [16, 40960], P('probe', 'blk')
- coeffs: float32 [2, 2, 16], P(None, None, 'probe')
The draws below stay inside these ranges and needn't reach their ends.
All inputs are finite; a program needn't handle non-finite values.
Results may differ from the reference program's by a relative error of at most 0.005.
Values may be sent and summed in bfloat16 or wider, within the bound.
No kernel may reach another device: no remote copies, remote signals or barrier semaphores. Data moves between devices by JAX's collectives and lax.ppermute only.
A program may use at most 64 MiB of HBM per device.

```python
import jax
import jax.numpy as jnp
from jax import lax

FEAT = 8
COLS = 16
ITERS = 2
ROWS_DEV = 640
PROBES = 15
POINTS = 40960
N_BLK = 64


def draw_targets(key, part):
    first_key = jax.random.fold_in(jax.random.fold_in(key, 7), 0)
    position = jnp.arange(POINTS, dtype=jnp.float32) / POINTS
    ramp = 0.5 + 1.5 * position
    return jnp.clip(jax.random.normal(first_key, (POINTS,), jnp.float32) * ramp, -8.0, 8.0)


def touch_ends(drawn, own_key, smallest, largest):
    longest = drawn.shape.index(max(drawn.shape))
    spots = []
    for shift in (0, 1):
        where = [jax.random.randint(jax.random.fold_in(own_key, axis), (), 0, length) for axis, length in enumerate(drawn.shape)]
        where[longest] = (where[longest] + shift) % drawn.shape[longest]
        spots.append(tuple(where))
    return drawn.at[spots[0]].set(smallest).at[spots[1]].set(largest)


def shard_levels(own_key, shape, cuts, smallest, top_value):
    loudness = 1.0
    for axis_at, blocks in cuts:
        draws = jax.random.uniform(jax.random.fold_in(jax.random.fold_in(own_key, 6), axis_at), (blocks,), jnp.float32, smallest / len(cuts), top_value / len(cuts))
        loudness = loudness * jnp.repeat(jnp.exp(draws), shape[axis_at] // blocks).reshape((-1,) + (1,) * (len(shape) - 1 - axis_at))
    return loudness


def centred(key, extent, scale, reach, pieces=(), kind=jnp.bfloat16):
    level = shard_levels(key, extent, pieces, -0.22, 0.18) if pieces else 1.0
    values = jax.random.normal(key, extent, jnp.float32) * scale * level
    return jnp.minimum(jnp.maximum(values, -reach), reach).astype(kind)


def setup_inputs(seed: int = 0) -> dict:
    arg_keys = jax.random.split(jax.random.key(seed), 4)
    return {
        "points": centred(arg_keys[0], (FEAT, POINTS), 1.0, 6.0, ((1, 256),), jnp.float32),
        "targets": draw_targets(jax.random.fold_in(arg_keys[3], 71), 0),
        "signs": touch_ends(jax.random.randint(arg_keys[2], (PROBES, POINTS), 0, 2), jax.random.fold_in(arg_keys[2], 1), 0, 1).astype(jnp.int32),
    }


def kernel_product(own_points, other_points, direction_bf):
    cross = lax.dot_general(other_points, own_points, (((0,), (0,)), ((), ())), precision=lax.Precision.HIGHEST, preferred_element_type=jnp.float32)
    norm_other = jnp.sum(other_points * other_points, 0)
    norm_own = jnp.sum(own_points * own_points, 0)
    squared = norm_other[:, None] + norm_own[None, :] - 2.0 * cross
    tile = jnp.exp(-0.5 * squared).astype(jnp.bfloat16)
    return jnp.dot(direction_bf, tile, preferred_element_type=jnp.float32)


def reference(points, targets, signs):
    rhs = jnp.concatenate([targets[None, :].astype(jnp.float32), 2.0 * signs.astype(jnp.float32) - 1.0], 0)

    def apply_kernel(direction):
        direction_bf = direction.astype(jnp.bfloat16)

        def one_block(block):
            own_points = lax.dynamic_slice_in_dim(points, (block * ROWS_DEV).astype(jnp.int32), ROWS_DEV, 1)
            return kernel_product(own_points, points, direction_bf)

        blocks = lax.map(one_block, jnp.arange(N_BLK, dtype=jnp.int32))
        return jnp.transpose(blocks, (1, 0, 2)).reshape(COLS, POINTS) + 0.5 * direction

    solution = jnp.zeros_like(rhs)
    residual = rhs
    direction = rhs
    norm_now = jnp.sum(residual * residual, 1)
    step_list = []
    ratio_list = []
    for iteration in range(ITERS):
        kernel_image = apply_kernel(direction)
        curvature = jnp.sum(direction * kernel_image, 1)
        step_size = norm_now / curvature
        solution = solution + step_size[:, None] * direction
        residual = residual - step_size[:, None] * kernel_image
        norm_next = jnp.sum(residual * residual, 1)
        dir_ratio = norm_next / norm_now
        direction = residual + dir_ratio[:, None] * direction
        norm_now = norm_next
        step_list.append(step_size)
        ratio_list.append(dir_ratio)
    coeffs = jnp.stack([jnp.stack(step_list), jnp.stack(ratio_list)])
    return (solution, residual, direction, coeffs)
```

```python
import jax
import jax.numpy as jnp
from jax import lax
from jax.experimental import pallas as pl
from jax.experimental.pallas import tpu as pltpu
from jax.sharding import PartitionSpec as P

COLS = 16
FEAT = 8
LANES = 128
DEPTH = 64
LOG2E = 1.4426950408889634


def split3(value):
    high = value.astype(jnp.bfloat16).astype(jnp.float32)
    rest = value - high
    mid = rest.astype(jnp.bfloat16).astype(jnp.float32)
    return high, mid, rest - mid


def norm_rows(norm, ones_first):
    high, mid, low = split3(norm)
    row = lax.broadcasted_iota(jnp.int32, (8, norm.shape[1]), 0)
    at = 3 if ones_first else 0
    value = jnp.where(row == at, high, jnp.where(row == at + 1, mid, jnp.where(row == at + 2, low, 0.0)))
    other = (row < 3) if ones_first else ((row >= 3) & (row < 6))
    return jnp.where(other, 1.0, value)


def left_rows(points):
    high, mid, low = split3(points)
    norm = (-0.5 * LOG2E) * jnp.sum(points * points, 0, keepdims=True)
    extra = norm_rows(norm, True)
    return jnp.concatenate([high, high, high, mid, mid, low, extra, jnp.zeros_like(extra)], 0)


def right_rows(points):
    high, mid, low = split3(points * LOG2E)
    norm = (-0.5 * LOG2E) * jnp.sum(points * points, 0, keepdims=True)
    extra = norm_rows(norm, False)
    return jnp.concatenate([high, mid, low, high, mid, high, extra, jnp.zeros_like(extra)], 0)


def join_rest(parts, group):
    lane = lax.broadcasted_iota(jnp.int32, (8, LANES), 1)
    out = None
    for at, part in enumerate(parts):
        turn = (32 * (at - group)) % LANES
        moved = pltpu.roll(part, turn, 1) if turn else part
        out = moved if out is None else jnp.where(lane >= 32 * at, moved, out)
    return out


def tile_kernel(own_ref, got_ref, tile_ref, image_ref, right_ref):
    rows = right_rows(own_ref[...])
    right_ref[...] = jnp.transpose(jnp.concatenate([rows, jnp.zeros_like(rows)], 0)).astype(jnp.bfloat16)
    image_ref[...] = jnp.zeros_like(image_ref)
    blocks = got_ref.shape[0]

    def step(points_list, rhs_list, offset):
        left = jnp.concatenate([left_rows(q) for q in points_list], 1).astype(jnp.bfloat16)
        rhs = jnp.concatenate(rhs_list, 1).astype(jnp.bfloat16)
        power = jnp.dot(right_ref[:, :DEPTH], left, preferred_element_type=jnp.float32)
        tile = jnp.exp2(power).astype(jnp.bfloat16)
        tile_ref[:, pl.ds(pl.multiple_of(offset, 2 * LANES), 2 * LANES)] = tile
        image_ref[...] += lax.dot_general(rhs, tile, (((1,), (1,)), ((), ())), preferred_element_type=jnp.float32)

    def main(pair, carry):
        first = 2 * pair
        step(
            [got_ref[first + k, 0:8, :] for k in range(2)],
            [got_ref[first + k, 8:24, :] for k in range(2)],
            pair * (2 * LANES),
        )
        return carry

    lax.fori_loop(0, blocks // 2, main, 0)

    def rest(pair, carry):
        points_list, rhs_list = [], []
        for k in range(2):
            parts = [got_ref[8 * pair + 4 * k + q, 24:32, :] for q in range(4)]
            points_list.append(join_rest(parts, 0))
            rhs_list.append(jnp.concatenate([join_rest(parts, 1), join_rest(parts, 2)], 0))
        step(points_list, rhs_list, (blocks + 2 * pair) * LANES)
        return carry

    lax.fori_loop(0, blocks // 8, rest, 0)


def totals(stats):
    curv = pltpu.roll(stats, LANES - 2, 2)
    quad = pltpu.roll(stats, LANES - 4, 2)
    left = pltpu.roll(stats, LANES - 6, 2)
    norm = jnp.sum(stats, 0)
    step = norm / jnp.sum(curv, 0)
    best = jnp.where(quad > 0.0, curv / jnp.where(quad > 0.0, quad, 1.0), 0.0)
    gap = step[None] - best
    ratio = jnp.sum(left + gap * gap * quad, 0) / norm
    column = lambda v: jnp.concatenate([v[:, 64:65], v[:, 65:66]], 0)
    return column(step), column(ratio)


def second_kernel(got_ref, image_ref, tile_ref, out_ref, coeff_ref, dir_ref):
    blocks = got_ref.shape[0]
    step, ratio = totals(image_ref[:, 16:24, :])
    lane = lax.broadcasted_iota(jnp.int32, (COLS, LANES), 1)
    coeff_ref[...] = jnp.where(lane == 0, step, jnp.where(lane == 1, ratio, 0.0))

    def put(rhs, image, block):
        new = (rhs - step * image) + ratio * rhs
        dir_ref[:, pl.ds(pl.multiple_of(block * LANES, LANES), LANES)] = new.astype(jnp.bfloat16)

    def main(block, carry):
        put(got_ref[block, 8:24, :], image_ref[block, 0:16, :], block)
        return carry

    lax.fori_loop(0, blocks, main, 0)

    def rest(group, carry):
        parts = [got_ref[4 * group + q, 24:32, :] for q in range(4)]
        images = [image_ref[4 * group + q, 16:24, :] for q in range(4)]
        put(
            jnp.concatenate([join_rest(parts, 1), join_rest(parts, 2)], 0),
            jnp.concatenate([join_rest(images, 0), join_rest(images, 1)], 0),
            blocks + group,
        )
        return carry

    lax.fori_loop(0, blocks // 4, rest, 0)

    out_ref[...] = jnp.zeros_like(out_ref)
    width = 1024

    def chunk(at, carry):
        cols = pl.ds(pl.multiple_of(at * width, width), width)
        out_ref[...] += lax.dot_general(
            dir_ref[:, cols], tile_ref[:, cols], (((1,), (1,)), ((), ())), preferred_element_type=jnp.float32
        )
        return carry

    lax.fori_loop(0, tile_ref.shape[1] // width, chunk, 0)


VMEM = pl.BlockSpec(memory_space=pltpu.VMEM)


def first_product(own, got):
    rows, points = own.shape[1], got.shape[0] * 160
    return pl.pallas_call(
        tile_kernel,
        out_shape=(
            jax.ShapeDtypeStruct((rows, points), jnp.bfloat16),
            jax.ShapeDtypeStruct((COLS, rows), jnp.float32),
        ),
        in_specs=[VMEM, VMEM],
        out_specs=(VMEM, VMEM),
        scratch_shapes=[pltpu.VMEM((rows, LANES), jnp.bfloat16)],
        compiler_params=pltpu.CompilerParams(vmem_limit_bytes=40 * 2**20),
        name="tile_product",
    )(own, got)


def second_product(got, image, tile):
    rows, points = tile.shape
    return pl.pallas_call(
        second_kernel,
        out_shape=(
            jax.ShapeDtypeStruct((COLS, rows), jnp.float32),
            jax.ShapeDtypeStruct((COLS, LANES), jnp.float32),
        ),
        in_specs=[VMEM, VMEM, VMEM],
        out_specs=(VMEM, VMEM),
        scratch_shapes=[pltpu.VMEM((COLS, points), jnp.bfloat16)],
        compiler_params=pltpu.CompilerParams(vmem_limit_bytes=40 * 2**20),
        name="second_product",
    )(got, image, tile)


def swap(value, bit):
    return lax.ppermute(value, "probe", [(i, i ^ bit) for i in range(4)])


def probe_total(value):
    value = value + swap(value, 1)
    return value + swap(value, 2)


def to_all_blocks(piece):
    blocks = lax.axis_size("blk")
    return lax.all_to_all(jnp.broadcast_to(piece[None], (blocks,) + piece.shape), "blk", 0, 0)


def side_by_side(groups):
    width = sum(g.shape[1] for g in groups)
    return jnp.concatenate([*groups, jnp.zeros((8, LANES - width), jnp.float32)], 1)


def block_sums(residual, image):
    norm = jnp.sum(residual * residual, 1, keepdims=True)
    curv = jnp.sum(residual * image, 1, keepdims=True)
    quad = jnp.sum(image * image, 1, keepdims=True)
    return norm, curv, quad


def on_device(points, targets, signs):
    place = lax.axis_index("probe")
    quarter = points.shape[1]
    rhs = jnp.concatenate([targets[None, :], 2.0 * signs.astype(jnp.float32) - 1.0], 0)
    lane = lax.broadcasted_iota(jnp.int32, (FEAT, 4 * quarter), 1)
    mine = jnp.where(lane // quarter == place, jnp.concatenate([points] * 4, 1), 0.0)
    own = probe_total(mine)

    def own_quarter(value):
        return lax.dynamic_slice_in_dim(value, place * quarter, quarter, 1)

    rhs_q = own_quarter(rhs)
    piece = jnp.concatenate(
        [
            points[:, :LANES],
            rhs_q[:, :LANES],
            side_by_side([points[:, LANES:], rhs_q[:8, LANES:], rhs_q[8:, LANES:]]),
        ],
        0,
    )
    got = to_all_blocks(piece)
    tile, partial = first_product(own, got)

    image = probe_total(partial) + 0.5 * rhs
    norm, curv, quad = block_sums(rhs, image)
    best = jnp.where(quad > 0.0, curv / jnp.where(quad > 0.0, quad, 1.0), 0.0)
    left = jnp.sum(jnp.square(rhs - best * image), 1, keepdims=True)
    image_q = own_quarter(image)
    stats = [part for value in (norm, curv, quad, left) for part in (value[:8], value[8:])]
    piece = jnp.concatenate(
        [image_q[:, :LANES], side_by_side([image_q[:8, LANES:], image_q[8:, LANES:], *stats])], 0
    )
    images = to_all_blocks(piece)
    partial, coeff = second_product(got, images, tile)

    step, ratio = coeff[:, 0:1], coeff[:, 1:2]
    residual = rhs - step * image
    direction = residual + ratio * rhs
    image = probe_total(partial) + 0.5 * direction
    norm = jnp.sum(residual * residual, 1, keepdims=True)
    curv = jnp.sum(direction * image, 1, keepdims=True)
    cross = jnp.sum(residual * image, 1, keepdims=True)
    quad = jnp.sum(image * image, 1, keepdims=True)
    best = jnp.where(quad > 0.0, cross / jnp.where(quad > 0.0, quad, 1.0), 0.0)
    left = jnp.sum(jnp.square(residual - best * image), 1, keepdims=True)
    stats = jnp.concatenate([norm, curv, quad, best, left], 1)
    stats = side_by_side([stats[:8], stats[8:]])
    sums = to_all_blocks(stats)
    sums = jnp.concatenate([sums[:, :, 0:5], sums[:, :, 5:10]], 1)
    norm_now = jnp.sum(sums[:, :, 0], 0)[:, None]
    step_two = norm_now / jnp.sum(sums[:, :, 1], 0)[:, None]
    gap = step_two[None, :, 0] - sums[:, :, 3]
    norm_next = jnp.sum(sums[:, :, 4] + gap * gap * sums[:, :, 2], 0)[:, None]
    ratio_two = norm_next / norm_now

    def own_cols(value):
        return lax.dynamic_slice_in_dim(value, place * 4, 4, 0)

    direction, image, residual, rhs = map(own_cols, (direction, image, residual, rhs))
    step, ratio, step_two, ratio_two = map(own_cols, (step, ratio, step_two, ratio_two))
    answer = step * rhs + step_two * direction
    residual = residual - step_two * image
    direction = residual + ratio_two * direction
    coeffs = jnp.stack([jnp.stack([step[:, 0], step_two[:, 0]]), jnp.stack([ratio[:, 0], ratio_two[:, 0]])])
    return (answer, residual, direction, coeffs)


def solution(mesh):
    placed = (P(None, ("blk", "probe")), P("blk"), P(None, "blk"))
    return jax.shard_map(
        on_device,
        mesh=mesh,
        in_specs=placed,
        out_specs=(P("probe", "blk"), P("probe", "blk"), P("probe", "blk"), P(None, None, "probe")),
        check_vma=False,
    )
```

```python
import jax
import jax.numpy as jnp
from jax import lax
from jax.experimental import pallas as pl
from jax.experimental.pallas import tpu as pltpu
from jax.sharding import PartitionSpec as P

COLS = 16
FEAT = 8
LANES = 128
REST = 32
DEPTH = 48
WIDTH = 1024
LOG2E = 1.4426950408889634
LIMIT = 24 * 2**20


def rounded(value):
    return value.astype(jnp.bfloat16).astype(jnp.float32)


def split3(value):
    high = rounded(value)
    mid = rounded(value - high)
    return high, mid, value - high - mid


def norm_rows(points, ones_first):
    high, mid, low = split3((-0.5 * LOG2E) * jnp.sum(points * points, 0, keepdims=True))
    row = lax.broadcasted_iota(jnp.int32, points.shape, 0)
    at = 3 if ones_first else 0
    value = jnp.where(row == at, high, jnp.where(row == at + 1, mid, jnp.where(row == at + 2, low, 0.0)))
    other = (row < 3) if ones_first else ((row >= 3) & (row < 6))
    return jnp.where(other, 1.0, value)


def left_rows(high, low):
    return jnp.concatenate([high, high, high, low, low, norm_rows(high + low, True)], 0)


def right_rows(points):
    high = rounded(points)
    points = high + rounded(points - high)
    top, mid, end = split3(points * LOG2E)
    return jnp.concatenate([top, mid, end, top, mid, norm_rows(points, False)], 0)


def lane_of(shape):
    return lax.broadcasted_iota(jnp.int32, shape, len(shape) - 1)


def turn(value, by):
    by = by % value.shape[-1]
    return pltpu.roll(value, by, value.ndim - 1) if by else value


def pack_rest(groups):
    lane = lane_of((8, LANES))
    out = jnp.zeros((8, LANES), jnp.float32)
    for at, group in enumerate(groups):
        out = jnp.where((lane >= REST * at) & (lane < REST * (at + 1)), turn(group, REST * at), out)
    return out


def join_rest(parts, group):
    lane = lane_of((8, LANES))
    out = None
    for at, part in enumerate(parts):
        moved = turn(part, REST * (at - group))
        out = moved if out is None else jnp.where(lane >= REST * at, moved, out)
    return out


def repeat_piece(ref, piece):
    piece = piece.astype(ref.dtype)

    def put(block, carry):
        ref[block] = piece
        return carry

    lax.fori_loop(0, ref.shape[0], put, 0, unroll=8)


def pack_kernel(place_ref, points_ref, targets_ref, signs_ref, piece_ref, rhs_ref, mine_ref):
    place = place_ref[0]
    quarter = points_ref.shape[1]
    rhs_ref[0:1, :] = targets_ref[...]
    rhs_ref[1:COLS, :] = 2.0 * signs_ref[...].astype(jnp.float32) - 1.0
    mine_ref[...] = jnp.zeros_like(mine_ref)
    mine_ref[:, 0:quarter] = points_ref[...]
    points = mine_ref[...]
    mine_ref[...] = pltpu.roll(points, place * quarter, 1)
    width = rhs_ref.shape[1]
    rhs = pltpu.roll(rhs_ref[...], lax.rem(width - place * quarter, width), 1)
    high = rounded(points)
    low = rounded(points - high)
    ends = slice(LANES, 2 * LANES)
    rest = pack_rest([rhs[:8, ends], rhs[8:, ends], high[:, ends], low[:, ends]])
    repeat_piece(
        piece_ref, jnp.concatenate([high[:, :LANES], low[:, :LANES], rhs[:, :LANES], rest], 0)
    )


def tile_kernel(own_ref, got_ref, tile_ref, image_ref, right_ref, left_ref, rhs_ref):
    rows = right_rows(own_ref[...])
    pad = jnp.zeros((LANES - DEPTH, rows.shape[1]), jnp.float32)
    right_ref[...] = jnp.transpose(jnp.concatenate([rows, pad], 0)).astype(jnp.bfloat16)
    blocks = got_ref.shape[0]

    def put(left, rhs, block):
        cols = pl.ds(pl.multiple_of(block * LANES, LANES), LANES)
        left_ref[:, cols] = left.astype(jnp.bfloat16)
        rhs_ref[:, cols] = rhs.astype(jnp.bfloat16)

    def main(block, carry):
        piece = got_ref[block].astype(jnp.float32)
        put(left_rows(piece[0:8], piece[8:16]), piece[16:32], block)
        return carry

    lax.fori_loop(0, blocks, main, 0, unroll=8)

    def rest(group, carry):
        parts = [got_ref[4 * group + q].astype(jnp.float32)[32:40] for q in range(4)]
        joined = [join_rest(parts, g) for g in range(4)]
        put(left_rows(joined[2], joined[3]), jnp.concatenate(joined[:2], 0), blocks + group)
        return carry

    lax.fori_loop(0, blocks // 4, rest, 0, unroll=4)

    def step(at, total):
        cols = pl.ds(pl.multiple_of(at * WIDTH, WIDTH), WIDTH)
        power = jnp.dot(right_ref[:, :DEPTH], left_ref[:, cols], preferred_element_type=jnp.float32)
        tile = jnp.exp2(power).astype(jnp.bfloat16)
        tile_ref[:, cols] = tile
        return total + lax.dot_general(
            rhs_ref[:, cols], tile, (((1,), (1,)), ((), ())), preferred_element_type=jnp.float32
        )

    image_ref[...] = lax.fori_loop(0, tile_ref.shape[1] // WIDTH, step, jnp.zeros(image_ref.shape, jnp.float32), unroll=2)


def safe_ratio(top, bottom):
    good = bottom > 0.0
    return jnp.where(good, top / jnp.where(good, bottom, 1.0), 0.0)


def row_sum(value):
    return jnp.sum(value, 1, keepdims=True)


def send_kernel(place_ref, rhs_ref, near_ref, far_ref, piece_ref, image_ref):
    rhs = rhs_ref[...]
    image = near_ref[...] + far_ref[...] + 0.5 * rhs
    image_ref[...] = image
    norm, curv, quad = row_sum(rhs * rhs), row_sum(rhs * image), row_sum(image * image)
    left = row_sum(jnp.square(rhs - safe_ratio(curv, quad) * image))
    share = safe_ratio(curv, norm)
    width = rhs.shape[1]
    back = lax.rem(width - place_ref[0] * (width // 4), width)
    rest = pltpu.roll(image - share * rhs, back, 1)
    packed = pack_rest([rest[:8, LANES : 2 * LANES], rest[8:, LANES : 2 * LANES]])
    lane = lane_of((8, LANES))
    at = 2 * REST
    for value in (norm, curv, quad, left, share):
        for part in split3(value):
            for half in (part[:8], part[8:]):
                packed = jnp.where(lane == at, half, packed)
                at += 1
    repeat_piece(piece_ref, jnp.concatenate([rest[:, :LANES], packed], 0))


def second_kernel(got_ref, images_ref, tile_ref, out_ref, coeff_ref, dir_ref):
    blocks = got_ref.shape[0]

    def add(block, sums):
        norm, curv = sums
        value = images_ref[block].astype(jnp.float32)[16:24]
        value = value + turn(value, -2) + turn(value, -4)
        return norm + value, curv + turn(value, -6)

    zero = jnp.zeros((8, LANES), jnp.float32)
    norm, curv = lax.fori_loop(0, blocks, add, (zero, zero), unroll=8)
    step = norm / curv

    def grow(block, total):
        value = images_ref[block].astype(jnp.float32)[16:24]
        value = value + turn(value, -2) + turn(value, -4)
        quad = turn(value, -12)
        gap = step - safe_ratio(turn(value, -6), quad)
        return total + turn(value, -18) + gap * gap * quad

    ratio = lax.fori_loop(0, blocks, grow, zero, unroll=8) / norm
    at = 2 * REST

    def column(value):
        return jnp.concatenate([value[:, at : at + 1], value[:, at + 1 : at + 2]], 0)

    step_col, ratio_col = column(step), column(ratio)
    lane = lane_of((COLS, LANES))
    coeff_ref[...] = jnp.where(lane == 0, step_col, jnp.where(lane == 1, ratio_col, 0.0))
    lane = lane_of((8, LANES))

    def factor(block):
        value = images_ref[block].astype(jnp.float32)[16:24]
        value = turn(value + turn(value, -2) + turn(value, -4), -24)
        return (1.0 + ratio_col) - step_col * column(value)

    def put(value, block):
        dir_ref[:, pl.ds(pl.multiple_of(block * LANES, LANES), LANES)] = value.astype(jnp.bfloat16)

    def group_of_four(group, carry):
        ends = []
        for q in range(4):
            block = 4 * group + q
            piece = got_ref[block].astype(jnp.float32)
            image = images_ref[block].astype(jnp.float32)
            scale = factor(block)
            put(scale * piece[16:32] - step_col * image[:16], block)
            low = lane < REST
            ends.append(
                jnp.where(low, scale[:8], scale[8:]) * piece[32:40]
                - jnp.where(low, step_col[:8], step_col[8:]) * image[16:24]
            )
        put(jnp.concatenate([join_rest(ends, 0), join_rest(ends, 1)], 0), blocks + group)
        return carry

    lax.fori_loop(0, blocks // 4, group_of_four, 0, unroll=2)

    def chunk(at, total):
        cols = pl.ds(pl.multiple_of(at * WIDTH, WIDTH), WIDTH)
        return total + lax.dot_general(
            dir_ref[:, cols], tile_ref[:, cols], (((1,), (1,)), ((), ())), preferred_element_type=jnp.float32
        )

    out_ref[...] = lax.fori_loop(0, tile_ref.shape[1] // WIDTH, chunk, jnp.zeros(out_ref.shape, jnp.float32), unroll=5)


def sums_kernel(rhs_ref, image_ref, coeff_ref, near_ref, far_ref, piece_ref, res_ref, dir_ref, out_ref):
    rhs = rhs_ref[...]
    step, ratio = coeff_ref[:, 0:1], coeff_ref[:, 1:2]
    residual = rhs - step * image_ref[...]
    direction = residual + ratio * rhs
    image = near_ref[...] + far_ref[...] + 0.5 * direction
    res_ref[...], dir_ref[...], out_ref[...] = residual, direction, image
    quad = row_sum(image * image)
    best = safe_ratio(row_sum(residual * image), quad)
    left = row_sum(jnp.square(residual - best * image))
    values = (row_sum(residual * residual), row_sum(direction * image), quad, best, left)
    lane = lane_of((8, LANES))
    piece = jnp.zeros((8, LANES), jnp.float32)
    for at, value in enumerate(values):
        piece = jnp.where(lane == 2 * at, value[:8], jnp.where(lane == 2 * at + 1, value[8:], piece))
    repeat_piece(piece_ref, piece)


def last_kernel(place_ref, sums_ref, rhs_ref, res_ref, dir_ref, image_ref, coeff_ref,
                answer_ref, residual_ref, direction_ref, coeffs_ref):
    sums = sums_ref[...]
    total = jnp.sum(sums, 0)
    step = total / turn(total, -2)
    gap = step[None] - turn(sums, -6)
    ratio = jnp.sum(turn(sums, -8) + gap * gap * turn(sums, -4), 0) / total

    def column(value):
        return jnp.concatenate([value[:, 0:1], value[:, 1:2]], 0)

    step, ratio = column(step), column(ratio)
    direction = dir_ref[...]
    residual = res_ref[...] - step * image_ref[...]

    def own_cols(value):
        out = value[0:4]
        for at in range(1, 4):
            out = jnp.where(place_ref[0] == at, value[4 * at : 4 * at + 4], out)
        return out

    answer_ref[...] = own_cols(coeff_ref[:, 0:1] * rhs_ref[...] + step * direction)
    residual_ref[...] = own_cols(residual)
    direction_ref[...] = own_cols(residual + ratio * direction)
    lane = lane_of((COLS, LANES))
    coeffs_ref[...] = own_cols(jnp.where(lane == 2, step, jnp.where(lane == 3, ratio, coeff_ref[...])))


VMEM = pl.BlockSpec(memory_space=pltpu.VMEM)
SMEM = pl.BlockSpec(memory_space=pltpu.SMEM)


def call(kernel, outs, scratch, *args):
    return pl.pallas_call(
        kernel,
        out_shape=tuple(jax.ShapeDtypeStruct(shape, kind) for shape, kind in outs),
        in_specs=[SMEM if a.dtype == jnp.int32 and a.shape == (1,) else VMEM for a in args],
        out_specs=tuple(VMEM for _ in outs),
        scratch_shapes=[pltpu.VMEM(shape, kind) for shape, kind in scratch],
        compiler_params=pltpu.CompilerParams(vmem_limit_bytes=LIMIT),
        name=kernel.__name__,
    )(*args)


def swap(value, bit):
    return lax.ppermute(value, "probe", [(i, i ^ bit) for i in range(4)])


def to_all_blocks(pieces):
    return lax.all_to_all(pieces, "blk", 0, 0)


def on_device(points, targets, signs):
    blocks = lax.axis_size("blk")
    rows = targets.shape[0]
    others = blocks * points.shape[1]
    place = lax.axis_index("probe").astype(jnp.int32)[None]
    f32, bf16 = jnp.float32, jnp.bfloat16
    wide = ((COLS, rows), f32)

    pieces, rhs, mine = call(
        pack_kernel,
        [((blocks, 40, LANES), bf16), wide, ((FEAT, rows), f32)],
        [],
        place, points, targets[None, :], signs,
    )
    got = to_all_blocks(pieces)
    own = mine + swap(mine, 1)
    own = own + swap(own, 2)
    tile, part = call(
        tile_kernel,
        [((rows, others), bf16), wide],
        [((rows, LANES), bf16), ((DEPTH, others), bf16), ((COLS, others), bf16)],
        own, got,
    )
    near = part + swap(part, 1)
    pieces, image = call(
        send_kernel, [((blocks, 24, LANES), bf16), wide], [], place, rhs, near, swap(near, 2)
    )
    images = to_all_blocks(pieces)
    part, coeff = call(
        second_kernel, [wide, ((COLS, LANES), f32)], [((COLS, others), bf16)], got, images, tile
    )
    near = part + swap(part, 1)
    pieces, residual, direction, image = call(
        sums_kernel, [((blocks, 8, LANES), f32), wide, wide, wide], [], rhs, image, coeff, near, swap(near, 2)
    )
    sums = to_all_blocks(pieces)
    small = ((4, rows), f32)
    answer, residual, direction, coeff = call(
        last_kernel,
        [small, small, small, ((4, LANES), f32)],
        [],
        place, sums, rhs, residual, direction, image, coeff,
    )
    coeffs = jnp.stack([coeff[:, 0:3:2].T, coeff[:, 1:4:2].T])
    return (answer, residual, direction, coeffs)


def solution(mesh):
    placed = (P(None, ("blk", "probe")), P("blk"), P(None, "blk"))
    return jax.shard_map(
        on_device,
        mesh=mesh,
        in_specs=placed,
        out_specs=(P("probe", "blk"), P("probe", "blk"), P("probe", "blk"), P(None, None, "probe")),
        check_vma=False,
    )
```

```python
import jax
import jax.numpy as jnp
from jax import lax
from jax.experimental import pallas as pl
from jax.experimental.pallas import tpu as pltpu
from jax.sharding import PartitionSpec as P

COLS = 16
FEAT = 8
LANES = 128
REST = 32
DEPTH = 48
WIDTH = 2560
LOG2E = 1.4426950408889634
LIMIT = 24 * 2**20


def rounded(value):
    return value.astype(jnp.bfloat16).astype(jnp.float32)


def split3(value):
    high = rounded(value)
    mid = rounded(value - high)
    return high, mid, value - high - mid


def norm_rows(points, ones_first):
    high, mid, low = split3((-0.5 * LOG2E) * jnp.sum(points * points, 0, keepdims=True))
    row = lax.broadcasted_iota(jnp.int32, points.shape, 0)
    at = 3 if ones_first else 0
    value = jnp.where(row == at, high, jnp.where(row == at + 1, mid, jnp.where(row == at + 2, low, 0.0)))
    other = (row < 3) if ones_first else ((row >= 3) & (row < 6))
    return jnp.where(other, 1.0, value)


def left_rows(high, low):
    return jnp.concatenate([high, high, high, low, low, norm_rows(high + low, True)], 0)


def right_rows(points):
    high = rounded(points)
    points = high + rounded(points - high)
    top, mid, end = split3(points * LOG2E)
    return jnp.concatenate([top, mid, end, top, mid, norm_rows(points, False)], 0)


def lane_of(shape):
    return lax.broadcasted_iota(jnp.int32, shape, len(shape) - 1)


def turn(value, by):
    by = by % value.shape[-1]
    return pltpu.roll(value, by, value.ndim - 1) if by else value


def pack_rest(groups):
    lane = lane_of((8, LANES))
    out = jnp.zeros((8, LANES), jnp.float32)
    for at, group in enumerate(groups):
        out = jnp.where((lane >= REST * at) & (lane < REST * (at + 1)), turn(group, REST * at), out)
    return out


def join_rest(parts, group):
    lane = lane_of((8, LANES))
    out = None
    for at, part in enumerate(parts):
        moved = turn(part, REST * (at - group))
        out = moved if out is None else jnp.where(lane >= REST * at, moved, out)
    return out


def repeat_piece(ref, piece):
    piece = piece.astype(ref.dtype)

    def put(block, carry):
        ref[block] = piece
        return carry

    lax.fori_loop(0, ref.shape[0], put, 0, unroll=8)


def pack_kernel(place_ref, points_hbm, targets_hbm, signs_hbm, piece_ref, mine_ref,
                points_ref, targets_ref, signs_ref, rhs_ref, wide_ref, sems):
    moves = [
        pltpu.make_async_copy(src, dst, sems.at[at])
        for at, (src, dst) in enumerate(
            ((points_hbm, points_ref), (targets_hbm, targets_ref), (signs_hbm, signs_ref))
        )
    ]
    for move in moves:
        move.start()
    for move in moves:
        move.wait()
    quarter = points_ref.shape[1]
    rhs_ref[0:1, :] = targets_ref[...][None, :]
    rhs_ref[1:COLS, :] = 2.0 * signs_ref[...].astype(jnp.float32) - 1.0
    wide_ref[:, 0:quarter] = points_ref[...]
    points = wide_ref[...]
    width = rhs_ref.shape[1]
    rhs = pltpu.roll(rhs_ref[...], lax.rem(width - place_ref[0] * quarter, width), 1)
    mine_ref[0:FEAT, :] = points_ref[...]
    mine_ref[FEAT : FEAT + COLS, :] = rhs[:, 0:quarter]
    high = rounded(points)
    low = rounded(points - high)
    ends = slice(LANES, 2 * LANES)
    rest = pack_rest([rhs[:8, ends], rhs[8:, ends], high[:, ends], low[:, ends]])
    repeat_piece(
        piece_ref, jnp.concatenate([high[:, :LANES], low[:, :LANES], rhs[:, :LANES], rest], 0)
    )


def tile_kernel(place_ref, near_ref, far_ref, got_ref, tile_ref, image_ref, sides_ref, left_ref, rhs_ref, wide_ref):
    place = place_ref[0]
    rows, quarter = near_ref.shape[0] // 2, near_ref.shape[1]
    wide_ref[...] = jnp.zeros_like(wide_ref)
    own = jnp.zeros(wide_ref.shape, jnp.float32)
    for flip in range(4):
        ref = near_ref if flip < 2 else far_ref
        first = rows * (flip % 2)
        wide_ref[:, 0:quarter] = ref[first : first + rows, :]
        own += pltpu.roll(wide_ref[...], jnp.bitwise_xor(place, flip) * quarter, 1)
    sides_ref[...] = own[FEAT:]
    right = right_rows(own[:FEAT]).astype(jnp.bfloat16)
    blocks = got_ref.shape[0]

    def left_and_rhs(block):
        if block < blocks:
            piece = got_ref[block].astype(jnp.float32)
            return left_rows(piece[0:8], piece[8:16]), piece[16:32]
        group = block - blocks
        parts = [got_ref[4 * group + q].astype(jnp.float32)[32:40] for q in range(4)]
        joined = [join_rest(parts, g) for g in range(4)]
        return left_rows(joined[2], joined[3]), jnp.concatenate(joined[:2], 0)

    total = jnp.zeros(image_ref.shape, jnp.float32)
    each = WIDTH // LANES
    for first in range(0, tile_ref.shape[0], WIDTH):
        for block in range(first // LANES, first // LANES + each):
            place = slice(block * LANES, (block + 1) * LANES)
            left, rhs = left_and_rhs(block)
            left_ref[place, :] = jnp.transpose(left).astype(jnp.bfloat16)
            rhs_ref[:, place] = rhs.astype(jnp.bfloat16)
        place = slice(first, first + WIDTH)
        power = jnp.dot(left_ref[place, :], right, preferred_element_type=jnp.float32)
        tile = jnp.exp2(power).astype(jnp.bfloat16)
        tile_ref[place, :] = tile
        total += jnp.dot(rhs_ref[:, place], tile, preferred_element_type=jnp.float32)
    image_ref[...] = total


def safe_ratio(top, bottom):
    good = bottom > 0.0
    return jnp.where(good, top / jnp.where(good, bottom, 1.0), 0.0)


def row_sum(value):
    return jnp.sum(value, 1, keepdims=True)


def send_kernel(place_ref, rhs_ref, near_ref, far_ref, piece_ref, image_ref):
    rhs = rhs_ref[...]
    image = near_ref[...] + far_ref[...] + 0.5 * rhs
    image_ref[...] = image
    norm, curv, quad = row_sum(rhs * rhs), row_sum(rhs * image), row_sum(image * image)
    best = safe_ratio(curv, quad)
    left = row_sum(jnp.square(rhs - best * image))
    share = safe_ratio(curv, norm)
    width = rhs.shape[1]
    back = lax.rem(width - place_ref[0] * (width // 4), width)
    rest = pltpu.roll(image - share * rhs, back, 1)
    packed = pack_rest([rest[:8, LANES : 2 * LANES], rest[8:, LANES : 2 * LANES]])
    lane = lane_of((8, LANES))
    at = 2 * REST
    for value in (norm, curv, quad, left, share, best):
        for part in split3(value):
            for half in (part[:8], part[8:]):
                packed = jnp.where(lane == at, half, packed)
                at += 1
    repeat_piece(piece_ref, jnp.concatenate([rest[:, :LANES], packed], 0))


def second_kernel(got_ref, images_ref, tile_ref, out_ref, coeff_ref, dir_ref, sums_ref):
    blocks = got_ref.shape[0]
    zero = jnp.zeros((8, LANES), jnp.float32)

    def add(block, total):
        value = images_ref[block].astype(jnp.float32)[16:24]
        value = value + turn(value, -2) + turn(value, -4)
        sums_ref[block] = value
        return total + value

    norm = lax.fori_loop(0, blocks, add, zero, unroll=16)
    step = norm / turn(norm, -6)

    def grow(block, total):
        value = sums_ref[block]
        gap = step - turn(value, -30)
        return total + turn(value, -18) + gap * gap * turn(value, -12)

    ratio = lax.fori_loop(0, blocks, grow, zero, unroll=16) / norm
    at = 2 * REST

    def column(value, at):
        return jnp.concatenate([value[:, at : at + 1], value[:, at + 1 : at + 2]], 0)

    step_col, ratio_col = column(step, at), column(ratio, at)
    lane = lane_of((COLS, LANES))
    coeff_ref[...] = jnp.where(lane == 0, step_col, jnp.where(lane == 1, ratio_col, 0.0))
    step_wide = jnp.broadcast_to(step_col, (COLS, LANES))
    grown = 1.0 + jnp.broadcast_to(ratio_col, (COLS, LANES))
    first = lane_of((8, LANES)) < REST
    step_rest = jnp.where(first, step_wide[:8], step_wide[8:])

    def put(value, block):
        dir_ref[:, block * LANES : (block + 1) * LANES] = value.astype(jnp.bfloat16)

    def product(first, width):
        return jnp.dot(
            dir_ref[:, first : first + width], tile_ref[first : first + width, :], preferred_element_type=jnp.float32
        )

    total = jnp.zeros(out_ref.shape, jnp.float32)
    for group in range(blocks // 4):
        ends = []
        for block in range(4 * group, 4 * group + 4):
            piece = got_ref[block].astype(jnp.float32)
            image = images_ref[block].astype(jnp.float32)
            scale = grown - step_wide * column(sums_ref[block], at + 24)
            put(scale * piece[16:32] - step_wide * image[:16], block)
            ends.append(jnp.where(first, scale[:8], scale[8:]) * piece[32:40] - step_rest * image[16:24])
        put(jnp.concatenate([join_rest(ends, 0), join_rest(ends, 1)], 0), blocks + group)
        if group % 4 == 3:
            total += product((group - 3) * 4 * LANES, 16 * LANES)
    out_ref[...] = total + product(blocks * LANES, blocks // 4 * LANES)


def sums_kernel(rhs_ref, image_ref, coeff_ref, near_ref, far_ref, piece_ref, res_ref, dir_ref, out_ref):
    rhs = rhs_ref[...]
    step, ratio = coeff_ref[:, 0:1], coeff_ref[:, 1:2]
    residual = rhs - step * image_ref[...]
    direction = residual + ratio * rhs
    image = near_ref[...] + far_ref[...] + 0.5 * direction
    res_ref[...], dir_ref[...], out_ref[...] = residual, direction, image
    quad = row_sum(image * image)
    best = safe_ratio(row_sum(residual * image), quad)
    left = row_sum(jnp.square(residual - best * image))
    values = (row_sum(residual * residual), row_sum(direction * image), quad, best, left)
    lane = lane_of((COLS, LANES))
    row = lax.broadcasted_iota(jnp.int32, (COLS, LANES), 0)
    piece = jnp.zeros((COLS, LANES), jnp.float32)
    for at, value in enumerate(values):
        piece = jnp.where(lane == row + COLS * at, value, piece)
    repeat_piece(piece_ref, jnp.sum(piece, 0, keepdims=True))


def last_kernel(place_ref, sums_ref, rhs_ref, res_ref, dir_ref, image_ref, coeff_ref,
                answer_ref, residual_ref, direction_ref, coeffs_ref):
    sums = sums_ref[:, 0, :]
    total = jnp.sum(sums, 0, keepdims=True)
    step_row = total / turn(total, -COLS)
    gap = step_row - turn(sums, -3 * COLS)
    grown = turn(sums, -4 * COLS) + gap * gap * turn(sums, -2 * COLS)
    ratio_row = jnp.sum(grown, 0, keepdims=True) / total
    lane = lane_of((COLS, LANES))
    row = lax.broadcasted_iota(jnp.int32, (COLS, LANES), 0)

    def column(value):
        return row_sum(jnp.where(lane == row, value, 0.0))

    step, ratio = column(step_row), column(ratio_row)
    first_step, first_ratio = coeff_ref[:, 0:1], coeff_ref[:, 1:2]
    direction = dir_ref[...]
    residual = res_ref[...] - step * image_ref[...]
    place = place_ref[0]

    def own_cols(value):
        out = value[0:4]
        for at in range(1, 4):
            out = jnp.where(place == at, value[4 * at : 4 * at + 4], out)
        return out

    answer_ref[...] = own_cols(first_step * rhs_ref[...] + step * direction)
    residual_ref[...] = own_cols(residual)
    direction_ref[...] = own_cols(residual + ratio * direction)
    for kind, values in enumerate(((first_step, step), (first_ratio, ratio))):
        for at, value in enumerate(values):
            picked = jnp.sum(jnp.where(lane == row - 4 * place, value, 0.0), 0, keepdims=True)
            coeffs_ref[kind, at : at + 1, :] = picked[:, 0:4]


VMEM = pl.BlockSpec(memory_space=pltpu.VMEM)
SMEM = pl.BlockSpec(memory_space=pltpu.SMEM)


def call(kernel, outs, scratch, *args, held=(), limit=LIMIT):
    kinds = [SMEM if a.shape == (1,) else pl.BlockSpec(memory_space=pltpu.HBM) if at in held else VMEM for at, a in enumerate(args)]
    return pl.pallas_call(
        kernel,
        out_shape=tuple(jax.ShapeDtypeStruct(shape, kind) for shape, kind in outs),
        in_specs=kinds,
        out_specs=tuple(VMEM for _ in outs),
        scratch_shapes=[pltpu.VMEM(*s) if isinstance(s, tuple) else s for s in scratch],
        compiler_params=pltpu.CompilerParams(vmem_limit_bytes=limit),
        name=kernel.__name__,
    )(*args)


def swap(value, bit):
    return lax.ppermute(value, "probe", [(i, i ^ bit) for i in range(4)])


def to_all_blocks(pieces):
    return lax.all_to_all(pieces, "blk", 0, 0)


def on_device(points, targets, signs):
    blocks = lax.axis_size("blk")
    rows = targets.shape[0]
    others = blocks * points.shape[1]
    place = lax.axis_index("probe").astype(jnp.int32)[None]
    f32, bf16 = jnp.float32, jnp.bfloat16
    wide = ((COLS, rows), f32)

    pieces, mine = call(
        pack_kernel,
        [((blocks, 40, LANES), bf16), ((FEAT + COLS, points.shape[1]), f32)],
        [
            (points.shape, f32), (targets.shape, f32), (signs.shape, signs.dtype), wide,
            ((FEAT, 2 * LANES), f32), pltpu.SemaphoreType.DMA((3,)),
        ],
        place, points, targets, signs,
        held=(1, 2, 3),
        limit=60 * 2**20,
    )
    got = to_all_blocks(pieces)
    near = jnp.concatenate([mine, swap(mine, 1)], 0)
    tile, part, rhs = call(
        tile_kernel,
        [((others, rows), bf16), wide, wide],
        [((others, DEPTH), bf16), ((COLS, others), bf16), ((FEAT + COLS, rows), f32)],
        place, near, swap(near, 2), got,
    )
    near = part + swap(part, 1)
    pieces, image = call(
        send_kernel, [((blocks, 24, LANES), bf16), wide], [], place, rhs, near, swap(near, 2)
    )
    images = to_all_blocks(pieces)
    part, coeff = call(
        second_kernel,
        [wide, ((COLS, LANES), f32)],
        [((COLS, others), bf16), ((blocks, 8, LANES), f32)],
        got, images, tile
    )
    near = part + swap(part, 1)
    pieces, residual, direction, image = call(
        sums_kernel, [((blocks, 1, LANES), f32), wide, wide, wide], [], rhs, image, coeff, near, swap(near, 2)
    )
    sums = to_all_blocks(pieces)
    small = ((4, rows), f32)
    answer, residual, direction, coeffs = call(
        last_kernel,
        [small, small, small, ((2, 2, 4), f32)],
        [],
        place, sums, rhs, residual, direction, image, coeff,
    )
    return (answer, residual, direction, coeffs)


def solution(mesh):
    placed = (P(None, ("blk", "probe")), P("blk"), P(None, "blk"))
    return jax.shard_map(
        on_device,
        mesh=mesh,
        in_specs=placed,
        out_specs=(P("probe", "blk"), P("probe", "blk"), P("probe", "blk"), P(None, None, "probe")),
        check_vma=False,
    )
```

```python
import jax
import jax.numpy as jnp
from jax import lax
from jax.experimental import pallas as pl
from jax.experimental.pallas import tpu as pltpu
from jax.sharding import PartitionSpec as P

COLS = 16
FEAT = 8
LANES = 128
REST = 32
DEPTH = 48
WIDTH = 2560
LOG2E = 1.4426950408889634
LIMIT = 24 * 2**20


def rounded(value):
    return value.astype(jnp.bfloat16).astype(jnp.float32)


def split3(value):
    high = rounded(value)
    mid = rounded(value - high)
    return high, mid, value - high - mid


def norm_rows(points, ones_first):
    high, mid, low = split3((-0.5 * LOG2E) * jnp.sum(points * points, 0, keepdims=True))
    row = lax.broadcasted_iota(jnp.int32, points.shape, 0)
    at = 3 if ones_first else 0
    value = jnp.where(row == at, high, jnp.where(row == at + 1, mid, jnp.where(row == at + 2, low, 0.0)))
    other = (row < 3) if ones_first else ((row >= 3) & (row < 6))
    return jnp.where(other, 1.0, value)


def left_rows(high, low):
    return jnp.concatenate([high, high, high, low, low, norm_rows(high + low, True)], 0)


def right_rows(points):
    high = rounded(points)
    points = high + rounded(points - high)
    top, mid, end = split3(points * LOG2E)
    return jnp.concatenate([top, mid, end, top, mid, norm_rows(points, False)], 0)


def lane_of(shape):
    return lax.broadcasted_iota(jnp.int32, shape, len(shape) - 1)


def turn(value, by):
    by = by % value.shape[-1]
    return pltpu.roll(value, by, value.ndim - 1) if by else value


def pack_rest(groups):
    lane = lane_of((8, LANES))
    out = jnp.zeros((8, LANES), jnp.float32)
    for at, group in enumerate(groups):
        out = jnp.where((lane >= REST * at) & (lane < REST * (at + 1)), turn(group, REST * at), out)
    return out


def join_rest(parts, group):
    lane = lane_of((8, LANES))
    out = None
    for at, part in enumerate(parts):
        moved = turn(part, REST * (at - group))
        out = moved if out is None else jnp.where(lane >= REST * at, moved, out)
    return out


def repeat_piece(ref, piece):
    piece = piece.astype(ref.dtype)

    def put(block, carry):
        ref[block] = piece
        return carry

    lax.fori_loop(0, ref.shape[0], put, 0, unroll=8)


def pack_kernel(place_ref, points_hbm, targets_hbm, signs_hbm, piece_ref, mine_ref,
                points_ref, targets_ref, signs_ref, rhs_ref, wide_ref, sems):
    moves = [
        pltpu.make_async_copy(src, dst, sems.at[at])
        for at, (src, dst) in enumerate(
            ((points_hbm, points_ref), (targets_hbm, targets_ref), (signs_hbm, signs_ref))
        )
    ]
    for move in moves:
        move.start()
    for move in moves:
        move.wait()
    quarter = points_ref.shape[1]
    rhs_ref[0:1, :] = targets_ref[...][None, :]
    rhs_ref[1:COLS, :] = 2.0 * signs_ref[...].astype(jnp.float32) - 1.0
    wide_ref[:, 0:quarter] = points_ref[...]
    points = wide_ref[...]
    width = rhs_ref.shape[1]
    rhs = pltpu.roll(rhs_ref[...], lax.rem(width - place_ref[0] * quarter, width), 1)
    mine_ref[0:FEAT, :] = points_ref[...]
    mine_ref[FEAT : FEAT + COLS, :] = rhs[:, 0:quarter]
    high = rounded(points)
    low = rounded(points - high)
    ends = slice(LANES, 2 * LANES)
    rest = pack_rest([rhs[:8, ends], rhs[8:, ends], high[:, ends], low[:, ends]])
    left = rhs[0:1] - rounded(rhs[0:1])
    row = lax.broadcasted_iota(jnp.int32, (8, LANES), 0)
    ends_left = jnp.where(lane_of((8, LANES)) < REST, left[:, ends], 0.0)
    left = jnp.where(row == 0, left[:, :LANES], jnp.where(row == 1, ends_left, 0.0))
    repeat_piece(
        piece_ref, jnp.concatenate([high[:, :LANES], low[:, :LANES], rhs[:, :LANES], rest, left], 0)
    )


def own_kernel(place_ref, near_ref, far_ref, right_ref, sides_ref, wide_ref):
    place = place_ref[0]
    rows, quarter = near_ref.shape[0] // 2, near_ref.shape[1]
    wide_ref[...] = jnp.zeros_like(wide_ref)
    own = jnp.zeros(wide_ref.shape, jnp.float32)
    for flip in range(4):
        ref = near_ref if flip < 2 else far_ref
        first = rows * (flip % 2)
        wide_ref[:, 0:quarter] = ref[first : first + rows, :]
        own += pltpu.roll(wide_ref[...], jnp.bitwise_xor(place, flip) * quarter, 1)
    sides_ref[...] = own[FEAT:]
    right_ref[...] = right_rows(own[:FEAT]).astype(jnp.bfloat16)


def tile_kernel(right_ref, got_ref, tile_ref, image_ref, left_ref, rhs_ref):
    right = right_ref[...]
    blocks = got_ref.shape[0]

    def left_and_rhs(block):
        if block < blocks:
            piece = got_ref[block].astype(jnp.float32)
            return left_rows(piece[0:8], piece[8:16]), piece[16:32]
        group = block - blocks
        parts = [got_ref[4 * group + q].astype(jnp.float32)[32:40] for q in range(4)]
        joined = [join_rest(parts, g) for g in range(4)]
        return left_rows(joined[2], joined[3]), jnp.concatenate(joined[:2], 0)

    total = jnp.zeros(image_ref.shape, jnp.float32)
    each = WIDTH // LANES
    for first in range(0, tile_ref.shape[0], WIDTH):
        for block in range(first // LANES, first // LANES + each):
            place = slice(block * LANES, (block + 1) * LANES)
            left, rhs = left_and_rhs(block)
            left_ref[place, :] = jnp.transpose(left).astype(jnp.bfloat16)
            rhs_ref[:, place] = rhs.astype(jnp.bfloat16)
        place = slice(first, first + WIDTH)
        power = jnp.dot(left_ref[place, :], right, preferred_element_type=jnp.float32)
        tile = jnp.exp2(power).astype(jnp.bfloat16)
        tile_ref[place, :] = tile
        total += jnp.dot(rhs_ref[:, place], tile, preferred_element_type=jnp.float32)
    image_ref[...] = total


def safe_ratio(top, bottom):
    good = bottom > 0.0
    return jnp.where(good, top / jnp.where(good, bottom, 1.0), 0.0)


def row_sum(value):
    return jnp.sum(value, 1, keepdims=True)


def send_kernel(place_ref, rhs_ref, near_ref, far_ref, piece_ref, image_ref):
    rhs = rhs_ref[...]
    image = near_ref[...] + far_ref[...] + 0.5 * rhs
    image_ref[...] = image
    norm, curv, quad = row_sum(rhs * rhs), row_sum(rhs * image), row_sum(image * image)
    best = safe_ratio(curv, quad)
    left = row_sum(jnp.square(rhs - best * image))
    share = safe_ratio(curv, norm)
    width = rhs.shape[1]
    back = lax.rem(width - place_ref[0] * (width // 4), width)
    rest = pltpu.roll(image - share * rhs, back, 1)
    packed = pack_rest([rest[:8, LANES : 2 * LANES], rest[8:, LANES : 2 * LANES]])
    lane = lane_of((8, LANES))
    at = 2 * REST
    for value in (norm, curv, quad, left, share, best):
        for part in split3(value):
            for half in (part[:8], part[8:]):
                packed = jnp.where(lane == at, half, packed)
                at += 1
    repeat_piece(piece_ref, jnp.concatenate([rest[:, :LANES], packed], 0))


def cols_of(value, place):
    out = value[0:4]
    for at in range(1, 4):
        out = jnp.where(place == at, value[4 * at : 4 * at + 4], out)
    return out


def second_kernel(place_ref, got_ref, images_ref, tile_ref, keep_ref, give_ref, coeff_ref, dir_ref, sums_ref):
    blocks = got_ref.shape[0]
    zero = jnp.zeros((8, LANES), jnp.float32)

    def add(block, total):
        value = images_ref[block].astype(jnp.float32)[16:24]
        value = value + turn(value, -2) + turn(value, -4)
        sums_ref[block] = value
        return total + value

    norm = lax.fori_loop(0, blocks, add, zero, unroll=16)
    step = norm / turn(norm, -6)

    def grow(block, total):
        value = sums_ref[block]
        gap = step - turn(value, -30)
        return total + turn(value, -18) + gap * gap * turn(value, -12)

    ratio = lax.fori_loop(0, blocks, grow, zero, unroll=16) / norm
    at = 2 * REST

    def column(value, at):
        return jnp.concatenate([value[:, at : at + 1], value[:, at + 1 : at + 2]], 0)

    step_col, ratio_col = column(step, at), column(ratio, at)
    lane = lane_of((COLS, LANES))
    coeff_ref[...] = jnp.where(lane == 0, step_col, jnp.where(lane == 1, ratio_col, 0.0))
    step_wide = jnp.broadcast_to(step_col, (COLS, LANES))
    grown = 1.0 + jnp.broadcast_to(ratio_col, (COLS, LANES))
    first = lane_of((8, LANES)) < REST
    step_rest = jnp.where(first, step_wide[:8], step_wide[8:])

    top = lax.broadcasted_iota(jnp.int32, (COLS, LANES), 0) == 0

    def put(value, block):
        dir_ref[:, block * LANES : (block + 1) * LANES] = value.astype(jnp.bfloat16)

    def product(first, width):
        return jnp.dot(
            dir_ref[:, first : first + width], tile_ref[first : first + width, :], preferred_element_type=jnp.float32
        )

    total = jnp.zeros((COLS, keep_ref.shape[1]), jnp.float32)
    for group in range(blocks // 4):
        ends = []
        for block in range(4 * group, 4 * group + 4):
            piece = got_ref[block].astype(jnp.float32)
            image = images_ref[block].astype(jnp.float32)
            scale = grown - step_wide * column(sums_ref[block], at + 24)
            main = piece[16:32] + jnp.where(top, piece[40:41], 0.0)
            ends_rhs = piece[32:40] + jnp.where(top[:8], piece[41:42], 0.0)
            put(scale * main - step_wide * image[:16], block)
            ends.append(jnp.where(first, scale[:8], scale[8:]) * ends_rhs - step_rest * image[16:24])
        put(jnp.concatenate([join_rest(ends, 0), join_rest(ends, 1)], 0), blocks + group)
        if group % 2 == 1:
            total += product((group - 1) * 4 * LANES, 8 * LANES)
    total += product(blocks * LANES, blocks // 4 * LANES)
    core = lax.rem(place_ref[0], 2)
    for ref, at in ((keep_ref, core), (give_ref, 1 - core)):
        ref[0:4, :], ref[4:8, :] = cols_of(total, at), cols_of(total, at + 2)


def sums_kernel(place_ref, rhs_ref, image_ref, coeff_ref, near_ref, far_ref,
                piece_ref, right_ref, res_ref, dir_ref, out_ref, steps_ref):
    place = place_ref[0]
    rhs, steps = cols_of(rhs_ref[...], place), cols_of(coeff_ref[...], place)
    residual = rhs - steps[:, 0:1] * cols_of(image_ref[...], place)
    direction = residual + steps[:, 1:2] * rhs
    image = jnp.where(place < 2, near_ref[0:4, :], near_ref[4:8, :]) + far_ref[...] + 0.5 * direction
    right_ref[...], steps_ref[...] = rhs, steps
    res_ref[...], dir_ref[...], out_ref[...] = residual, direction, image
    quad = row_sum(image * image)
    best = safe_ratio(row_sum(residual * image), quad)
    left = row_sum(jnp.square(residual - best * image))
    values = (row_sum(residual * residual), row_sum(direction * image), quad, best, left)
    lane = lane_of((4, LANES))
    row = lax.broadcasted_iota(jnp.int32, (4, LANES), 0)
    piece = jnp.zeros((4, LANES), jnp.float32)
    for at, value in enumerate(values):
        piece = jnp.where(lane == row + 4 * at, value, piece)
    repeat_piece(piece_ref, jnp.sum(piece, 0, keepdims=True))


def last_kernel(sums_ref, right_ref, res_ref, dir_ref, image_ref, steps_ref,
                answer_ref, residual_ref, direction_ref, coeffs_ref):
    sums = sums_ref[:, 0, :]
    total = jnp.sum(sums, 0, keepdims=True)
    step_row = total / turn(total, -4)
    gap = step_row - turn(sums, -12)
    grown = turn(sums, -16) + gap * gap * turn(sums, -8)
    ratio_row = jnp.sum(grown, 0, keepdims=True) / total
    lane = lane_of((4, LANES))
    row = lax.broadcasted_iota(jnp.int32, (4, LANES), 0)

    def column(value):
        return row_sum(jnp.where(lane == row, value, 0.0))

    step, ratio = column(step_row), column(ratio_row)
    first_step, first_ratio = steps_ref[:, 0:1], steps_ref[:, 1:2]
    direction = dir_ref[...]
    residual = res_ref[...] - step * image_ref[...]
    answer_ref[...] = first_step * right_ref[...] + step * direction
    residual_ref[...] = residual
    direction_ref[...] = residual + ratio * direction
    for kind, values in enumerate(((first_step, step), (first_ratio, ratio))):
        for at, value in enumerate(values):
            picked = jnp.sum(jnp.where(lane == row, value, 0.0), 0, keepdims=True)
            coeffs_ref[kind, at : at + 1, :] = picked[:, 0:4]


VMEM = pl.BlockSpec(memory_space=pltpu.VMEM)
SMEM = pl.BlockSpec(memory_space=pltpu.SMEM)


def call(kernel, outs, scratch, *args, held=(), limit=LIMIT):
    kinds = [SMEM if a.shape == (1,) else pl.BlockSpec(memory_space=pltpu.HBM) if at in held else VMEM for at, a in enumerate(args)]
    return pl.pallas_call(
        kernel,
        out_shape=tuple(jax.ShapeDtypeStruct(shape, kind) for shape, kind in outs),
        in_specs=kinds,
        out_specs=tuple(VMEM for _ in outs),
        scratch_shapes=[pltpu.VMEM(*s) if isinstance(s, tuple) else s for s in scratch],
        compiler_params=pltpu.CompilerParams(vmem_limit_bytes=limit),
        name=kernel.__name__,
    )(*args)


def swap(value, bit):
    return lax.ppermute(value, "probe", [(i, i ^ bit) for i in range(4)])


def to_all_blocks(pieces):
    return lax.all_to_all(pieces, "blk", 0, 0)


def on_device(points, targets, signs):
    blocks = lax.axis_size("blk")
    rows = targets.shape[0]
    others = blocks * points.shape[1]
    place = lax.axis_index("probe").astype(jnp.int32)[None]
    f32, bf16 = jnp.float32, jnp.bfloat16
    wide = ((COLS, rows), f32)

    pieces, mine = call(
        pack_kernel,
        [((blocks, 48, LANES), bf16), ((FEAT + COLS, points.shape[1]), f32)],
        [
            (points.shape, f32), (targets.shape, f32), (signs.shape, signs.dtype), wide,
            ((FEAT, 2 * LANES), f32), pltpu.SemaphoreType.DMA((3,)),
        ],
        place, points, targets, signs,
        held=(1, 2, 3),
        limit=60 * 2**20,
    )
    got = to_all_blocks(pieces)
    near = jnp.concatenate([mine, swap(mine, 1)], 0)
    right, rhs = call(
        own_kernel, [((DEPTH, rows), bf16), wide], [((FEAT + COLS, rows), f32)], place, near, swap(near, 2)
    )
    tile, part = call(
        tile_kernel,
        [((others, rows), bf16), wide],
        [((others, DEPTH), bf16), ((COLS, others), bf16)],
        right, got,
    )
    near = part + swap(part, 1)
    pieces, image = call(
        send_kernel, [((blocks, 24, LANES), f32), wide], [], place, rhs, near, swap(near, 2)
    )
    images = to_all_blocks(pieces)
    keep, give, coeff = call(
        second_kernel,
        [((8, rows), f32), ((8, rows), f32), ((COLS, LANES), f32)],
        [((COLS, others), bf16), ((blocks, 8, LANES), f32)],
        place, got, images, tile,
    )
    near = keep + swap(give, 1)
    far = swap(jnp.where(place[0] < 2, near[4:], near[:4]), 2)
    small = ((4, rows), f32)
    pieces, rhs, residual, direction, image, steps = call(
        sums_kernel,
        [((blocks, 1, LANES), f32), small, small, small, small, ((4, LANES), f32)],
        [],
        place, rhs, image, coeff, near, far,
    )
    sums = to_all_blocks(pieces)
    answer, residual, direction, coeffs = call(
        last_kernel,
        [small, small, small, ((2, 2, 4), f32)],
        [],
        sums, rhs, residual, direction, image, steps,
    )
    return (answer, residual, direction, coeffs)


def solution(mesh):
    placed = (P(None, ("blk", "probe")), P("blk"), P(None, "blk"))
    return jax.shard_map(
        on_device,
        mesh=mesh,
        in_specs=placed,
        out_specs=(P("probe", "blk"), P("probe", "blk"), P("probe", "blk"), P(None, None, "probe")),
        check_vma=False,
    )
```

```python
import jax
import jax.numpy as jnp
from jax import lax
from jax.experimental import pallas as pl
from jax.experimental.pallas import tpu as pltpu
from jax.sharding import PartitionSpec as P

COLS = 16
FEAT = 8
LANES = 128
REST = 32
DEPTH = 48
WIDTH = 2560
LOG2E = 1.4426950408889634
LIMIT = 24 * 2**20


def rounded(value):
    return value.astype(jnp.bfloat16).astype(jnp.float32)


def split3(value):
    high = rounded(value)
    mid = rounded(value - high)
    return high, mid, value - high - mid


def norm_rows(points, ones_first):
    high, mid, low = split3((-0.5 * LOG2E) * jnp.sum(points * points, 0, keepdims=True))
    row = lax.broadcasted_iota(jnp.int32, points.shape, 0)
    at = 3 if ones_first else 0
    value = jnp.where(row == at, high, jnp.where(row == at + 1, mid, jnp.where(row == at + 2, low, 0.0)))
    other = (row < 3) if ones_first else ((row >= 3) & (row < 6))
    return jnp.where(other, 1.0, value)


def left_rows(high, low):
    return jnp.concatenate([high, high, high, low, low, norm_rows(high + low, True)], 0)


def right_rows(points):
    high = rounded(points)
    points = high + rounded(points - high)
    top, mid, end = split3(points * LOG2E)
    return jnp.concatenate([top, mid, end, top, mid, norm_rows(points, False)], 0)


def lane_of(shape):
    return lax.broadcasted_iota(jnp.int32, shape, len(shape) - 1)


def turn(value, by):
    by = by % value.shape[-1]
    return pltpu.roll(value, by, value.ndim - 1) if by else value


def pack_rest(groups):
    lane = lane_of((8, LANES))
    out = jnp.zeros((8, LANES), jnp.float32)
    for at, group in enumerate(groups):
        out = jnp.where((lane >= REST * at) & (lane < REST * (at + 1)), turn(group, REST * at), out)
    return out


def join_rest(parts, group):
    lane = lane_of((8, LANES))
    out = None
    for at, part in enumerate(parts):
        moved = turn(part, REST * (at - group))
        out = moved if out is None else jnp.where(lane >= REST * at, moved, out)
    return out


def repeat_piece(ref, piece):
    piece = piece.astype(ref.dtype)

    def put(block, carry):
        ref[block] = piece
        return carry

    lax.fori_loop(0, ref.shape[0], put, 0, unroll=8)


def pack_kernel(place_ref, points_hbm, targets_hbm, signs_hbm, piece_ref, mine_ref,
                points_ref, targets_ref, signs_ref, rhs_ref, wide_ref, sems):
    moves = [
        pltpu.make_async_copy(src, dst, sems.at[at])
        for at, (src, dst) in enumerate(
            ((points_hbm, points_ref), (targets_hbm, targets_ref), (signs_hbm, signs_ref))
        )
    ]
    for move in moves:
        move.start()
    for move in moves:
        move.wait()
    quarter = points_ref.shape[1]
    rhs_ref[0:1, :] = targets_ref[...][None, :]
    rhs_ref[1:COLS, :] = 2.0 * signs_ref[...].astype(jnp.float32) - 1.0
    wide_ref[:, 0:quarter] = points_ref[...]
    points = wide_ref[...]
    width = rhs_ref.shape[1]
    rhs = pltpu.roll(rhs_ref[...], lax.rem(width - place_ref[0] * quarter, width), 1)
    mine_ref[0:FEAT, :] = points_ref[...]
    mine_ref[FEAT : FEAT + COLS, :] = rhs[:, 0:quarter]
    high = rounded(points)
    low = rounded(points - high)
    ends = slice(LANES, 2 * LANES)
    rest = pack_rest([rhs[:8, ends], rhs[8:, ends], high[:, ends], low[:, ends]])
    left = rhs[0:1] - rounded(rhs[0:1])
    row = lax.broadcasted_iota(jnp.int32, (8, LANES), 0)
    ends_left = jnp.where(lane_of((8, LANES)) < REST, left[:, ends], 0.0)
    left = jnp.where(row == 0, left[:, :LANES], jnp.where(row == 1, ends_left, 0.0))
    repeat_piece(
        piece_ref, jnp.concatenate([high[:, :LANES], low[:, :LANES], rhs[:, :LANES], rest, left], 0)
    )


def own_kernel(place_ref, near_ref, far_ref, right_ref, sides_ref, wide_ref):
    place = place_ref[0]
    rows, quarter = near_ref.shape[0] // 2, near_ref.shape[1]
    wide_ref[...] = jnp.zeros_like(wide_ref)
    own = jnp.zeros(wide_ref.shape, jnp.float32)
    for flip in range(4):
        ref = near_ref if flip < 2 else far_ref
        first = rows * (flip % 2)
        wide_ref[:, 0:quarter] = ref[first : first + rows, :]
        own += pltpu.roll(wide_ref[...], jnp.bitwise_xor(place, flip) * quarter, 1)
    sides_ref[...] = own[FEAT:]
    right_ref[...] = right_rows(own[:FEAT]).astype(jnp.bfloat16)


def tile_kernel(right_ref, got_ref, tile_ref, image_ref, left_ref, rhs_ref):
    right = right_ref[...]
    blocks = got_ref.shape[0]

    def left_and_rhs(block):
        if block < blocks:
            piece = got_ref[block].astype(jnp.float32)
            return left_rows(piece[0:8], piece[8:16]), piece[16:32]
        group = block - blocks
        parts = [got_ref[4 * group + q].astype(jnp.float32)[32:40] for q in range(4)]
        joined = [join_rest(parts, g) for g in range(4)]
        return left_rows(joined[2], joined[3]), jnp.concatenate(joined[:2], 0)

    total = jnp.zeros(image_ref.shape, jnp.float32)
    each = WIDTH // LANES
    for first in range(0, tile_ref.shape[0], WIDTH):
        for block in range(first // LANES, first // LANES + each):
            place = slice(block * LANES, (block + 1) * LANES)
            left, rhs = left_and_rhs(block)
            left_ref[place, :] = jnp.transpose(left).astype(jnp.bfloat16)
            rhs_ref[:, place] = rhs.astype(jnp.bfloat16)
        place = slice(first, first + WIDTH)
        power = jnp.dot(left_ref[place, :], right, preferred_element_type=jnp.float32)
        tile = jnp.exp2(power).astype(jnp.bfloat16)
        tile_ref[place, :] = tile
        total += jnp.dot(rhs_ref[:, place], tile, preferred_element_type=jnp.float32)
    image_ref[...] = total


def safe_ratio(top, bottom):
    good = bottom > 0.0
    return jnp.where(good, top / jnp.where(good, bottom, 1.0), 0.0)


def row_sum(value):
    return jnp.sum(value, 1, keepdims=True)


def send_kernel(place_ref, rhs_ref, near_ref, far_ref, piece_ref, image_ref):
    rhs = rhs_ref[...]
    image = near_ref[...] + far_ref[...] + 0.5 * rhs
    image_ref[...] = image
    norm, curv, quad = row_sum(rhs * rhs), row_sum(rhs * image), row_sum(image * image)
    best = safe_ratio(curv, quad)
    left = row_sum(jnp.square(rhs - best * image))
    share = safe_ratio(curv, norm)
    width = rhs.shape[1]
    back = lax.rem(width - place_ref[0] * (width // 4), width)
    rest = pltpu.roll(image - share * rhs, back, 1)
    packed = pack_rest([rest[:8, LANES : 2 * LANES], rest[8:, LANES : 2 * LANES]])
    lane = lane_of((8, LANES))
    at = 2 * REST
    for value in (norm, curv, quad, left, share, best):
        for part in split3(value):
            for half in (part[:8], part[8:]):
                packed = jnp.where(lane == at, half, packed)
                at += 1
    piece = jnp.concatenate([rest[:, :LANES], packed], 0)
    repeat_piece(piece_ref, jnp.concatenate([rounded(piece), piece - rounded(piece)], 0))


def cols_of(value, place):
    out = value[0:4]
    for at in range(1, 4):
        out = jnp.where(place == at, value[4 * at : 4 * at + 4], out)
    return out


def second_kernel(place_ref, got_ref, images_ref, tile_ref, keep_ref, give_ref, coeff_ref, dir_ref, sums_ref):
    blocks = got_ref.shape[0]
    zero = jnp.zeros((8, LANES), jnp.float32)

    def add(block, total):
        value = images_ref[block].astype(jnp.float32)[16:24]
        value = value + turn(value, -2) + turn(value, -4)
        sums_ref[block] = value
        return total + value

    norm = lax.fori_loop(0, blocks, add, zero, unroll=16)
    step = norm / turn(norm, -6)

    def grow(block, total):
        value = sums_ref[block]
        gap = step - turn(value, -30)
        return total + turn(value, -18) + gap * gap * turn(value, -12)

    ratio = lax.fori_loop(0, blocks, grow, zero, unroll=16) / norm
    at = 2 * REST

    def column(value, at):
        return jnp.concatenate([value[:, at : at + 1], value[:, at + 1 : at + 2]], 0)

    step_col, ratio_col = column(step, at), column(ratio, at)
    lane = lane_of((COLS, LANES))
    coeff_ref[...] = jnp.where(lane == 0, step_col, jnp.where(lane == 1, ratio_col, 0.0))
    step_wide = jnp.broadcast_to(step_col, (COLS, LANES))
    grown = 1.0 + jnp.broadcast_to(ratio_col, (COLS, LANES))
    first = lane_of((8, LANES)) < REST
    step_rest = jnp.where(first, step_wide[:8], step_wide[8:])

    top = lax.broadcasted_iota(jnp.int32, (COLS, LANES), 0) == 0

    def put(value, block):
        dir_ref[:, block * LANES : (block + 1) * LANES] = value.astype(jnp.bfloat16)

    def product(first, width):
        return jnp.dot(
            dir_ref[:, first : first + width], tile_ref[first : first + width, :], preferred_element_type=jnp.float32
        )

    total = jnp.zeros((COLS, keep_ref.shape[1]), jnp.float32)
    for group in range(blocks // 4):
        ends = []
        for block in range(4 * group, 4 * group + 4):
            piece = got_ref[block].astype(jnp.float32)
            image = images_ref[block].astype(jnp.float32)
            image = image[:24] + image[24:]
            scale = grown - step_wide * column(sums_ref[block], at + 24)
            main = piece[16:32] + jnp.where(top, piece[40:41], 0.0)
            ends_rhs = piece[32:40] + jnp.where(top[:8], piece[41:42], 0.0)
            put(scale * main - step_wide * image[:16], block)
            ends.append(jnp.where(first, scale[:8], scale[8:]) * ends_rhs - step_rest * image[16:24])
        put(jnp.concatenate([join_rest(ends, 0), join_rest(ends, 1)], 0), blocks + group)
        if group % 2 == 1:
            total += product((group - 1) * 4 * LANES, 8 * LANES)
    total += product(blocks * LANES, blocks // 4 * LANES)
    core = lax.rem(place_ref[0], 2)
    for ref, at in ((keep_ref, core), (give_ref, 1 - core)):
        ref[0:4, :], ref[4:8, :] = cols_of(total, at), cols_of(total, at + 2)


def sums_kernel(place_ref, rhs_ref, image_ref, coeff_ref, near_ref, far_ref,
                piece_ref, right_ref, res_ref, dir_ref, out_ref, steps_ref):
    place = place_ref[0]
    rhs, steps = cols_of(rhs_ref[...], place), cols_of(coeff_ref[...], place)
    residual = rhs - steps[:, 0:1] * cols_of(image_ref[...], place)
    direction = residual + steps[:, 1:2] * rhs
    image = jnp.where(place < 2, near_ref[0:4, :], near_ref[4:8, :]) + far_ref[...] + 0.5 * direction
    right_ref[...], steps_ref[...] = rhs, steps
    res_ref[...], dir_ref[...], out_ref[...] = residual, direction, image
    quad = row_sum(image * image)
    best = safe_ratio(row_sum(residual * image), quad)
    left = row_sum(jnp.square(residual - best * image))
    values = (row_sum(residual * residual), row_sum(direction * image), quad, best, left)
    lane = lane_of((4, LANES))
    row = lax.broadcasted_iota(jnp.int32, (4, LANES), 0)
    piece = jnp.zeros((4, LANES), jnp.float32)
    for at, value in enumerate(values):
        piece = jnp.where(lane == row + 4 * at, value, piece)
    repeat_piece(piece_ref, jnp.sum(piece, 0, keepdims=True))


def last_kernel(sums_ref, right_ref, res_ref, dir_ref, image_ref, steps_ref,
                answer_ref, residual_ref, direction_ref, coeffs_ref):
    sums = sums_ref[:, 0, :]
    total = jnp.sum(sums, 0, keepdims=True)
    step_row = total / turn(total, -4)
    gap = step_row - turn(sums, -12)
    grown = turn(sums, -16) + gap * gap * turn(sums, -8)
    ratio_row = jnp.sum(grown, 0, keepdims=True) / total
    lane = lane_of((4, LANES))
    row = lax.broadcasted_iota(jnp.int32, (4, LANES), 0)

    def column(value):
        return row_sum(jnp.where(lane == row, value, 0.0))

    step, ratio = column(step_row), column(ratio_row)
    first_step, first_ratio = steps_ref[:, 0:1], steps_ref[:, 1:2]
    direction = dir_ref[...]
    residual = res_ref[...] - step * image_ref[...]
    answer_ref[...] = first_step * right_ref[...] + step * direction
    residual_ref[...] = residual
    direction_ref[...] = residual + ratio * direction
    for kind, values in enumerate(((first_step, step), (first_ratio, ratio))):
        for at, value in enumerate(values):
            picked = jnp.sum(jnp.where(lane == row, value, 0.0), 0, keepdims=True)
            coeffs_ref[kind, at : at + 1, :] = picked[:, 0:4]


VMEM = pl.BlockSpec(memory_space=pltpu.VMEM)
SMEM = pl.BlockSpec(memory_space=pltpu.SMEM)


def call(kernel, outs, scratch, *args, held=(), limit=LIMIT):
    kinds = [SMEM if a.shape == (1,) else pl.BlockSpec(memory_space=pltpu.HBM) if at in held else VMEM for at, a in enumerate(args)]
    return pl.pallas_call(
        kernel,
        out_shape=tuple(jax.ShapeDtypeStruct(shape, kind) for shape, kind in outs),
        in_specs=kinds,
        out_specs=tuple(VMEM for _ in outs),
        scratch_shapes=[pltpu.VMEM(*s) if isinstance(s, tuple) else s for s in scratch],
        compiler_params=pltpu.CompilerParams(vmem_limit_bytes=limit),
        name=kernel.__name__,
    )(*args)


def swap(value, bit):
    return lax.ppermute(value, "probe", [(i, i ^ bit) for i in range(4)])


def to_all_blocks(pieces):
    return lax.all_to_all(pieces, "blk", 0, 0)


def on_device(points, targets, signs):
    blocks = lax.axis_size("blk")
    rows = targets.shape[0]
    others = blocks * points.shape[1]
    place = lax.axis_index("probe").astype(jnp.int32)[None]
    f32, bf16 = jnp.float32, jnp.bfloat16
    wide = ((COLS, rows), f32)

    pieces, mine = call(
        pack_kernel,
        [((blocks, 48, LANES), bf16), ((FEAT + COLS, points.shape[1]), f32)],
        [
            (points.shape, f32), (targets.shape, f32), (signs.shape, signs.dtype), wide,
            ((FEAT, 2 * LANES), f32), pltpu.SemaphoreType.DMA((3,)),
        ],
        place, points, targets, signs,
        held=(1, 2, 3),
        limit=60 * 2**20,
    )
    got = to_all_blocks(pieces)
    near = jnp.concatenate([mine, swap(mine, 1)], 0)
    right, rhs = call(
        own_kernel, [((DEPTH, rows), bf16), wide], [((FEAT + COLS, rows), f32)], place, near, swap(near, 2)
    )
    tile, part = call(
        tile_kernel,
        [((others, rows), bf16), wide],
        [((others, DEPTH), bf16), ((COLS, others), bf16)],
        right, got,
    )
    near = part + swap(part, 1)
    pieces, image = call(
        send_kernel, [((blocks, 48, LANES), bf16), wide], [], place, rhs, near, swap(near, 2)
    )
    images = to_all_blocks(pieces)
    keep, give, coeff = call(
        second_kernel,
        [((8, rows), f32), ((8, rows), f32), ((COLS, LANES), f32)],
        [((COLS, others), bf16), ((blocks, 8, LANES), f32)],
        place, got, images, tile,
    )
    near = keep + swap(give, 1)
    far = swap(jnp.where(place[0] < 2, near[4:], near[:4]), 2)
    small = ((4, rows), f32)
    pieces, rhs, residual, direction, image, steps = call(
        sums_kernel,
        [((blocks, 1, LANES), f32), small, small, small, small, ((4, LANES), f32)],
        [],
        place, rhs, image, coeff, near, far,
    )
    sums = to_all_blocks(pieces)
    answer, residual, direction, coeffs = call(
        last_kernel,
        [small, small, small, ((2, 2, 4), f32)],
        [],
        sums, rhs, residual, direction, image, steps,
    )
    return (answer, residual, direction, coeffs)


def solution(mesh):
    placed = (P(None, ("blk", "probe")), P("blk"), P(None, "blk"))
    return jax.shard_map(
        on_device,
        mesh=mesh,
        in_specs=placed,
        out_specs=(P("probe", "blk"), P("probe", "blk"), P("probe", "blk"), P(None, None, "probe")),
        check_vma=False,
    )
```
